32 devices in a mesh: mem: 8 (over y, x, core), head: 4 (over z).
Axes of the slice: x: 2, y: 2, z: 4, core: 2. Of those that a mesh axis runs over, the one named last changes fastest.
Arguments:
- queries: bfloat16 [1024, 4096], P('mem', 'head'), may hold values from -200 to 200
- mem_keys: bfloat16 [768, 4096], P('mem', 'head'), may hold values from -6 to 6
- mem_values: bfloat16 [768, 4096], P('mem', 'head'), may hold values from -24 to 24
- own_values: bfloat16 [1024, 4096], P('mem', 'head'), may hold values from -6 to 6
- gate_bias: float32 [32], P('head'), may hold values from -2 to 2
- w_out: bfloat16 [4096, 4096], P('head'), may hold values from -0.09375 to 0.09375
- probes: int32 [1024, 8], P('mem'), may hold values from 0 to 47, as said below
- pattern: int32 [8, 8], replicated, may hold values from 0 to 1, as said below
Outputs:
- projected: bfloat16 [1024, 4096], P(('mem', 'head'))
The draws below stay inside these ranges and needn't reach their ends.
Inputs may be any that keep to these rules, and one draw needn't show every extreme that they name: `pattern`: entries are 0 or 1; every row has at least one 1. `probes`: the 8 clusters of a query are distinct. The first lies in a cluster block b with pattern[r, b] = 1, r being the query's block of 128 rows.
All inputs are finite; a program needn't handle non-finite values.
Results may differ from the reference program's by a relative error of at most 0.012.
Values may be sent and summed in bfloat16 or wider, within the bound.
A program may use at most 128 MiB of HBM per device.

```python
import math
import jax
import jax.numpy as jnp
from jax import lax

HEADS = 32
HD = 128
D = 4096
QDEV = 128
CSIZE = 16
PROBES = 8
BLOCKS = 8
CL_DEV = 6
CLUSTERS = 48
Q = 1024
MEM = 768


def make_all(key):
    keys_list = [jax.random.fold_in(key, 101 + number) for number in range(8)]
    level = 2 ** jax.random.randint(keys_list[0], (BLOCKS, 1), 0, 4)
    pattern = (jax.random.randint(keys_list[1], (BLOCKS, BLOCKS), 0, 8) < level).astype(jnp.int32)
    forced = jax.random.randint(keys_list[2], (BLOCKS, 1), 0, BLOCKS)
    block_ids = jnp.arange(BLOCKS, dtype=jnp.int32)
    pattern = jnp.maximum(pattern, (block_ids[None, :] == forced).astype(jnp.int32))
    anchor = jnp.arange(Q, dtype=jnp.int32) // QDEV
    row_allowed = pattern[anchor]
    block_score = row_allowed * 2 ** 24 + jax.random.randint(keys_list[3], (Q, BLOCKS), 0, 2 ** 14) * BLOCKS + block_ids[None, :]
    unused, first_block = lax.top_k(block_score, 1)
    first = first_block[:, 0] * CL_DEV + jax.random.randint(keys_list[4], (Q,), 0, CL_DEV)
    cluster_ids = jnp.arange(CLUSTERS, dtype=jnp.int32)
    cluster_score = jax.random.randint(keys_list[5], (Q, CLUSTERS), 0, 2 ** 14) * CLUSTERS + cluster_ids[None, :]
    cluster_score = jnp.where(cluster_ids[None, :] == first[:, None], -1, cluster_score)
    unused_too, others = lax.top_k(cluster_score, PROBES - 1)
    probes = jnp.concatenate([first[:, None], others], axis=1).astype(jnp.int32)
    mem_keys = jnp.clip(jax.random.normal(keys_list[6], (MEM, D), jnp.float32), -6.0, 6.0)
    queries = jnp.clip(jax.random.normal(keys_list[7], (Q, D), jnp.float32), -6.0, 6.0)
    return (pattern, probes, queries, mem_keys)


def draw_pattern(key, part):
    return make_all(key)[0]


def draw_probes(key, part):
    return make_all(key)[1]


def draw_queries(key, part):
    return make_all(key)[2].astype(jnp.bfloat16)


def draw_mem_keys(key, part):
    return make_all(key)[3].astype(jnp.bfloat16)


def block_scale(stream_key, dims, cuts, low, largest):
    def one(dim, parts):
        draws = jax.random.uniform(jax.random.fold_in(jax.random.fold_in(stream_key, 6), dim), (parts,), jnp.float32, low / len(cuts), largest / len(cuts))
        return jnp.repeat(jnp.exp(draws), dims[dim] // parts).reshape((-1,) + (1,) * (len(dims) - dim - 1))

    gain = one(*cuts[0])
    for cut in cuts[1:]:
        gain = gain * one(*cut)
    return gain


def noise(key, extent, scale, most, split=(), kind=jnp.bfloat16):
    loudness = block_scale(key, extent, split, -0.22, 0.18) if split else 1.0
    entries = jax.random.normal(key, extent, jnp.float32) * scale * loudness
    return jnp.minimum(jnp.maximum(entries, -most), most).astype(kind)


def setup_inputs(seed: int = 0) -> dict:
    key_list = jax.random.split(jax.random.key(seed), 9)
    return {
        "queries": draw_queries(jax.random.fold_in(key_list[8], 71), 0),
        "mem_keys": draw_mem_keys(jax.random.fold_in(key_list[8], 71), 0),
        "mem_values": noise(key_list[2], (MEM, D), 4.0, 24.0, ((0, 8), (1, 4))),
        "own_values": noise(key_list[3], (Q, D), 1.0, 6.0, ((0, 8), (1, 4))),
        "gate_bias": jnp.clip(jax.random.uniform(key_list[4], (HEADS,), jnp.float32, -2.0, 2.0) * block_scale(key_list[4], (HEADS,), ((0, 4),), -0.4, 0.0), -2.0, 2.0),
        "w_out": noise(key_list[5], (D, D), D ** -0.5, 0.09375, ((0, 4),)),
        "probes": draw_probes(jax.random.fold_in(key_list[8], 71), 0),
        "pattern": draw_pattern(jax.random.fold_in(key_list[8], 71), 0),
    }


def reference(queries, mem_keys, mem_values, own_values, gate_bias, w_out, probes, pattern):
    cluster_ids = jnp.arange(CLUSTERS, dtype=jnp.int32)
    probed = jnp.any(probes[:, :, None] == cluster_ids[None, None, :], axis=1)
    allowed = jnp.repeat(pattern, CL_DEV, axis=1) > 0
    keys_all = mem_keys.astype(jnp.float32).reshape(MEM, HEADS, HD)
    vals_all = mem_values.astype(jnp.float32).reshape(MEM, HEADS, HD)
    gate = jax.nn.sigmoid(gate_bias.astype(jnp.float32))[None, :, None]
    score_scale = 1.0 / math.sqrt(HD)

    def one_block(block):
        first_row = (block * QDEV).astype(jnp.int32)
        query_block = lax.dynamic_slice_in_dim(queries, first_row, QDEV, 0).astype(jnp.float32).reshape(QDEV, HEADS, HD)
        probe_block = lax.dynamic_slice_in_dim(probed, first_row, QDEV, 0)
        allowed_row = lax.dynamic_index_in_dim(allowed, block, 0, keepdims=False)
        cluster_mask = probe_block & allowed_row[None, :]
        entry_mask = jnp.repeat(cluster_mask, CSIZE, axis=1).T
        scores = jnp.einsum('khd,qhd->hkq', keys_all, query_block) * score_scale
        scores = jnp.where(entry_mask[None], scores, -jnp.inf)
        row_peak = lax.optimization_barrier(jnp.max(scores, axis=1))
        weights = jnp.where(entry_mask[None], jnp.exp(scores - row_peak[:, None, :]), 0.0)
        denominator = lax.optimization_barrier(jnp.sum(weights, axis=1))
        rounded = lax.optimization_barrier(weights.astype(jnp.bfloat16)).astype(jnp.float32)
        recalled = jnp.einsum('hkq,khd->qhd', rounded, vals_all) / denominator.T[:, :, None]
        own_part = lax.dynamic_slice_in_dim(own_values, first_row, QDEV, 0).astype(jnp.float32).reshape(QDEV, HEADS, HD)
        blended = (gate * recalled + (1.0 - gate) * own_part).reshape(QDEV, HEADS * HD).astype(jnp.bfloat16)
        return jnp.dot(blended, w_out, preferred_element_type=jnp.float32).astype(jnp.bfloat16)
    outputs = lax.map(one_block, jnp.arange(BLOCKS, dtype=jnp.int32))
    return outputs.reshape(BLOCKS * QDEV, HEADS * HD)
```

```python
import functools
import math

import jax
import jax.numpy as jnp
from jax import lax
from jax.experimental import pallas as pl
from jax.experimental.pallas import tpu as pltpu
from jax.sharding import PartitionSpec as P

HD = 128
CSIZE = 16
PIECES = 4
NEG = -1e30
MESH = pl.DeviceIdType.MESH


def row_orders(n):
    orders = []
    for z in range(n):
        ups = list(range(n - 1, z, -1))
        downs = list(range(z))
        first, second = (ups, downs) if len(ups) >= len(downs) else (downs, ups)
        order = []
        while first or second:
            if first:
                order.append(first.pop(0))
            if second:
                order.append(second.pop(0))
        orders.append(order + [z])
    return orders


def kernel(
    n_mem, n_head, heads, q_hbm, k_hbm, v_hbm, own_hbm, gate_ref, w_hbm, probes_ref, pattern_ref,
    out_ref,
    q_all, k_all, v_all, p_all, p_mine, onehot, o_send, recalled, own, w, blend, part, part_send, part_recv,
    kv_send, kv_recv, q_send, q_recv, o_send_sem, o_recv_sem, p_send, p_recv, r_send, r_recv, w_sem, local_sem,
):
    qdev = q_all.shape[1]
    kdev = k_hbm.shape[0]
    width = w.shape[1] // PIECES
    rows = qdev // n_head
    nq = heads * rows
    entries = k_all.shape[0]
    clusters = onehot.shape[1]
    per_block = kdev // CSIZE
    me = lax.axis_index("mem")
    z = lax.axis_index("head")
    group = me // heads
    j = me % heads
    base = group * heads

    barrier = pltpu.get_barrier_semaphore()
    for d in range(1, n_mem):
        pl.semaphore_signal(barrier, inc=1, device_id=((me + d) % n_mem, z), device_id_type=MESH)

    @pl.when(z > 0)
    def _():
        pl.semaphore_signal(barrier, inc=1, device_id=(me, z - 1), device_id_type=MESH)

    @pl.when(z < n_head - 1)
    def _():
        pl.semaphore_signal(barrier, inc=1, device_id=(me, z + 1), device_id_type=MESH)

    orders = row_orders(n_head)
    turn = []
    for s in range(n_head):
        t = jnp.int32(orders[0][s])
        for zz in range(1, n_head):
            t = jnp.where(z == zz, orders[zz][s], t)
        turn.append(t)

    def cols(head):
        return pl.ds(pl.multiple_of(head * HD, HD), HD)

    def at_rows(t):
        return pl.ds(pl.multiple_of(t * rows, rows), rows)

    def src_rows(src):
        return pl.ds(pl.multiple_of(src * kdev, kdev), kdev)

    locals_ = [
        pltpu.make_async_copy(k_hbm.at[:, cols(j)], k_all.at[src_rows(me)], local_sem.at[0]),
        pltpu.make_async_copy(q_hbm.at[:, cols(j)], q_all.at[j], local_sem.at[1]),
        pltpu.make_async_copy(v_hbm.at[:, cols(j)], v_all.at[src_rows(me)], local_sem.at[2]),
        pltpu.make_async_copy(own_hbm, own, local_sem.at[3]),
    ]
    for copy in locals_:
        copy.start()

    mine = probes_ref[...]
    allowed = jnp.zeros_like(mine)
    for b in range(n_mem):
        inside = (mine >= b * per_block) & (mine < (b + 1) * per_block)
        allowed = jnp.where(inside, pattern_ref[me, b], allowed)
    mine = jnp.where(allowed > 0, mine, -1)
    p_mine[...] = mine
    p_all[j] = mine
    onehot[...] = (
        lax.broadcasted_iota(jnp.int32, (entries, clusters), 0) // CSIZE
        == lax.broadcasted_iota(jnp.int32, (entries, clusters), 1)
    ).astype(jnp.float32).astype(jnp.bfloat16)

    neighbours = jnp.where(z > 0, 1, 0) + jnp.where(z < n_head - 1, 1, 0)
    pl.semaphore_wait(barrier, n_mem - 1 + neighbours)

    sends = []

    def send(src, dst, send_sem, recv_sem, device):
        copy = pltpu.make_async_remote_copy(
            src_ref=src, dst_ref=dst, send_sem=send_sem, recv_sem=recv_sem,
            device_id=device, device_id_type=MESH,
        )
        copy.start()
        sends.append(copy)

    def arrived(ref, recv_sem):
        pltpu.make_async_remote_copy(
            src_ref=ref, dst_ref=ref, send_sem=kv_send.at[0, 0], recv_sem=recv_sem,
            device_id=((me + 1) % n_mem, z), device_id_type=MESH,
        ).wait_recv()

    def send_kv(kind, source, target):
        for d in range(1, n_mem):
            to = (me + d) % n_mem
            send(source.at[:, cols(to % heads)], target.at[src_rows(me)],
                 kv_send.at[kind, d], kv_recv.at[kind, me], (to, z))

    def send_q(s):
        for d in range(1, heads):
            to = (j + d) % heads
            send(q_hbm.at[at_rows(turn[s]), cols(to)], q_all.at[j, at_rows(turn[s])],
                 q_send.at[s, d], q_recv.at[s, j], (base + to, z))

    for d in range(1, heads):
        send(p_mine, p_all.at[j], p_send.at[d], p_recv.at[j], (base + (j + d) % heads, z))
    send_kv(0, k_hbm, k_all)
    send_q(0)
    send_kv(1, v_hbm, v_all)
    for s in range(1, n_head):
        send_q(s)
    w_copies = []
    for c in range(PIECES):
        span = pl.ds(c * width, width)
        copy = pltpu.make_async_copy(w_hbm.at[:, span], w.at[:, span], w_sem.at[c])
        copy.start()
        w_copies.append(copy)

    def wait_kv(kind, target):
        for d in range(1, n_mem):
            src = (me + n_mem - d) % n_mem
            arrived(target.at[src_rows(src)], kv_recv.at[kind, src])

    scale = math.log2(math.e) / math.sqrt(HD)
    per_tile = HD // rows
    own_backs = []

    def attend(s):
        t = turn[s]
        if s == 0:
            for d in range(1, heads):
                src = (j + heads - d) % heads
                arrived(p_all.at[src], p_recv.at[src])
            locals_[0].wait()
            locals_[1].wait()
            wait_kv(0, k_all)
        for d in range(1, heads):
            src = (j + heads - d) % heads
            arrived(q_all.at[src, at_rows(t)], q_recv.at[s, src])
        lane = lax.broadcasted_iota(jnp.int32, (p_all.shape[1], qdev), 1) // rows
        tiles = []
        for first in range(0, heads, per_tile):
            tile = jnp.zeros((p_all.shape[1], qdev), jnp.int32)
            for k in range(per_tile):
                shift = (k * rows + qdev - t * rows) % qdev
                tile = jnp.where(lane == k, pltpu.roll(p_all[first + k], shift, 1), tile)
            tiles.append(tile)
        probed = jnp.concatenate(tiles, axis=1)
        ids = lax.broadcasted_iota(jnp.int32, (clusters, nq), 0)
        bias = jnp.full((clusters, nq), NEG, jnp.float32)
        for k in range(p_all.shape[1]):
            bias = jnp.where(probed[k : k + 1, :] == ids, 0.0, bias)
        block = q_all[:, at_rows(t), :].reshape(nq, HD)
        scores = lax.dot_general(
            k_all[...], block, (((1,), (1,)), ((), ())), preferred_element_type=jnp.float32
        ) + jnp.dot(onehot[...], bias.astype(jnp.bfloat16), preferred_element_type=jnp.float32)
        peak = jnp.max(scores, axis=0, keepdims=True)
        weights = jnp.exp2((scores - peak) * scale)
        denominator = jnp.sum(weights, axis=0, keepdims=True)
        if s == 0:
            locals_[2].wait()
            wait_kv(1, v_all)
        got = lax.dot_general(
            v_all[...], weights.astype(jnp.bfloat16), (((0,), (0,)), ((), ())),
            preferred_element_type=jnp.float32,
        )
        got = got * (1.0 / denominator)
        o_send[s] = got.T.astype(jnp.bfloat16)
        for d in range(1, heads):
            to = (j + d) % heads
            send(o_send.at[s, at_rows(to)], recalled.at[j, at_rows(t)],
                 o_send_sem.at[s, d], o_recv_sem.at[s, j], (base + to, z))
        back = pltpu.make_async_copy(
            o_send.at[s, at_rows(j)], recalled.at[j, at_rows(t)], o_recv_sem.at[s, j])
        back.start()
        own_backs.append(back)

    def project(s):
        t = turn[s]
        own_backs[s].wait()
        for d in range(1, heads):
            src = (j + heads - d) % heads
            arrived(recalled.at[src, at_rows(t)], o_recv_sem.at[s, src])
        if s == 0:
            locals_[3].wait()
        for h in range(heads):
            gate = 1.0 / (1.0 + jnp.exp(-jnp.full((1, HD), gate_ref[h], jnp.float32)))
            mixed = gate * recalled[h, at_rows(t), :].astype(jnp.float32) + (1.0 - gate) * own[
                at_rows(t), h * HD : (h + 1) * HD
            ].astype(jnp.float32)
            blend[:, h * HD : (h + 1) * HD] = mixed.astype(jnp.bfloat16)
        up = t > z
        for c in range(PIECES):
            span = pl.ds(c * width, width)
            if s == 0:
                w_copies[c].wait()
            part[...] = jnp.dot(blend[...], w[:, span], preferred_element_type=jnp.float32)
            if s < n_head - 1:
                has_prev = jnp.where(up, z, n_head - 1 - z) > 0

                @pl.when(has_prev)
                def _():
                    arrived(part_recv.at[t, :, span], r_recv.at[t, c])
                    part[...] += part_recv[t, :, span].astype(jnp.float32)

                part_send[s, :, span] = part[...].astype(jnp.bfloat16)
                to = jnp.where(up, z + 1, z - 1)
                slot = jnp.where(t == z - 1, n_head, t)
                send(part_send.at[s, :, span], part_recv.at[slot, :, span],
                     r_send.at[s, c], r_recv.at[slot, c], (me, to))
            else:

                @pl.when(z > 0)
                def _():
                    arrived(part_recv.at[z, :, span], r_recv.at[z, c])
                    part[...] += part_recv[z, :, span].astype(jnp.float32)

                @pl.when(z < n_head - 1)
                def _():
                    arrived(part_recv.at[n_head, :, span], r_recv.at[n_head, c])
                    part[...] += part_recv[n_head, :, span].astype(jnp.float32)

                out_ref[:, span] = part[...].astype(out_ref.dtype)

    attend(0)
    for s in range(1, n_head):
        attend(s)
        project(s - 1)
    project(n_head - 1)
    for copy in sends:
        copy.wait_send()


def solution(mesh):
    n_mem, n_head = mesh.shape["mem"], mesh.shape["head"]

    def local(queries, mem_keys, mem_values, own_values, gate_bias, w_out, probes, pattern):
        qdev, feats = queries.shape
        kdev = mem_keys.shape[0]
        heads = feats // HD
        width = w_out.shape[1]
        rows = qdev // n_head
        entries = n_mem * kdev
        bf16, f32 = jnp.bfloat16, jnp.float32
        anywhere = pl.BlockSpec(memory_space=pl.ANY)
        smem = pl.BlockSpec(memory_space=pltpu.SMEM)
        vmem = pl.BlockSpec(memory_space=pltpu.VMEM)
        dma = pltpu.SemaphoreType.DMA
        return pl.pallas_call(
            functools.partial(kernel, n_mem, n_head, heads),
            out_shape=jax.ShapeDtypeStruct((rows, width), bf16),
            in_specs=[anywhere, anywhere, anywhere, anywhere, smem, anywhere, vmem, smem],
            out_specs=vmem,
            scratch_shapes=[
                pltpu.VMEM((heads, qdev, HD), bf16),
                pltpu.VMEM((entries, HD), bf16),
                pltpu.VMEM((entries, HD), bf16),
                pltpu.VMEM((heads, probes.shape[1], qdev), jnp.int32),
                pltpu.VMEM((probes.shape[1], qdev), jnp.int32),
                pltpu.VMEM((entries, entries // CSIZE), bf16),
                pltpu.VMEM((n_head, heads * rows, HD), bf16),
                pltpu.VMEM((heads, qdev, HD), bf16),
                pltpu.VMEM((qdev, feats), bf16),
                pltpu.VMEM((feats, width), bf16),
                pltpu.VMEM((rows, feats), bf16),
                pltpu.VMEM((rows, width // PIECES), f32),
                pltpu.VMEM((n_head, rows, width), bf16),
                pltpu.VMEM((n_head + 1, rows, width), bf16),
                dma((2, n_mem)), dma((2, n_mem)),
                dma((n_head, heads)), dma((n_head, heads)),
                dma((n_head, heads)), dma((n_head, heads)),
                dma((heads,)), dma((heads,)),
                dma((n_head, PIECES)), dma((n_head + 1, PIECES)),
                dma((PIECES,)), dma((4,)),
            ],
            compiler_params=pltpu.CompilerParams(
                collective_id=0, has_side_effects=True, vmem_limit_bytes=56 * 2**20
            ),
            cost_estimate=pl.CostEstimate(
                flops=2 * qdev * feats * width, bytes_accessed=2 * feats * width, transcendentals=0
            ),
        )(queries, mem_keys, mem_values, own_values, gate_bias, w_out, probes.T, pattern)

    in_specs = (
        P("mem", "head"),
        P("mem", "head"),
        P("mem", "head"),
        P("mem", "head"),
        P("head"),
        P("head", None),
        P("mem", None),
        P(),
    )
    out_specs = P(("mem", "head"), None)
    return jax.shard_map(local, mesh=mesh, in_specs=in_specs, out_specs=out_specs, check_vma=False)
```

```python
import functools
import math

import jax
import jax.numpy as jnp
from jax import lax
from jax.experimental import pallas as pl
from jax.experimental.pallas import tpu as pltpu
from jax.sharding import PartitionSpec as P

HD = 128
CSIZE = 16
PIECES = 4
NEG = -1e30
MESH = pl.DeviceIdType.MESH


def row_orders(n):
    orders = []
    for z in range(n):
        ups = list(range(n - 1, z, -1))
        downs = list(range(z))
        first, second = (ups, downs) if len(ups) >= len(downs) else (downs, ups)
        order = []
        while first or second:
            if first:
                order.append(first.pop(0))
            if second:
                order.append(second.pop(0))
        orders.append(order + [z])
    return orders


def kernel(
    n_mem, n_head, heads, q_hbm, k_hbm, v_hbm, own_hbm, gate_ref, w_hbm, probes_ref, pattern_ref,
    out_ref,
    q_all, k_all, v_all, p_all, p_mine, onehot, o_send, recalled, own, w, blend, part, part_send, part_recv,
    kv_send, kv_recv, q_send, q_recv, o_send_sem, o_recv_sem, p_send, p_recv, r_send, r_recv, w_sem, local_sem,
):
    qdev = q_all.shape[1]
    kdev = k_hbm.shape[0]
    width = w.shape[1] // PIECES
    rows = qdev // n_head
    nq = heads * rows
    entries = k_all.shape[0]
    clusters = onehot.shape[1]
    per_block = kdev // CSIZE
    me = lax.axis_index("mem")
    z = lax.axis_index("head")
    group = me // heads
    j = me % heads
    base = group * heads

    barrier = pltpu.get_barrier_semaphore()
    for d in range(1, n_mem):
        pl.semaphore_signal(barrier, inc=1, device_id=((me + d) % n_mem, z), device_id_type=MESH)

    @pl.when(z > 0)
    def _():
        pl.semaphore_signal(barrier, inc=1, device_id=(me, z - 1), device_id_type=MESH)

    @pl.when(z < n_head - 1)
    def _():
        pl.semaphore_signal(barrier, inc=1, device_id=(me, z + 1), device_id_type=MESH)

    orders = row_orders(n_head)
    turn = []
    for s in range(n_head):
        t = jnp.int32(orders[0][s])
        for zz in range(1, n_head):
            t = jnp.where(z == zz, orders[zz][s], t)
        turn.append(t)

    def cols(head):
        return pl.ds(pl.multiple_of(head * HD, HD), HD)

    def at_rows(t):
        return pl.ds(pl.multiple_of(t * rows, rows), rows)

    def src_rows(src):
        return pl.ds(pl.multiple_of(src * kdev, kdev), kdev)

    locals_ = [
        pltpu.make_async_copy(k_hbm.at[:, cols(j)], k_all.at[src_rows(me)], local_sem.at[0]),
        pltpu.make_async_copy(q_hbm.at[:, cols(j)], q_all.at[j], local_sem.at[1]),
        pltpu.make_async_copy(v_hbm.at[:, cols(j)], v_all.at[src_rows(me)], local_sem.at[2]),
        pltpu.make_async_copy(own_hbm, own, local_sem.at[3]),
    ]
    for copy in locals_:
        copy.start()

    mine = probes_ref[...]
    allowed = jnp.zeros_like(mine)
    for b in range(n_mem):
        inside = (mine >= b * per_block) & (mine < (b + 1) * per_block)
        allowed = jnp.where(inside, pattern_ref[me, b], allowed)
    mine = jnp.where(allowed > 0, mine, -1)
    p_mine[...] = mine
    p_all[j] = mine
    onehot[...] = (
        lax.broadcasted_iota(jnp.int32, (entries, clusters), 0) // CSIZE
        == lax.broadcasted_iota(jnp.int32, (entries, clusters), 1)
    ).astype(jnp.float32).astype(jnp.bfloat16)

    neighbours = jnp.where(z > 0, 1, 0) + jnp.where(z < n_head - 1, 1, 0)
    pl.semaphore_wait(barrier, n_mem - 1 + neighbours)

    sends = []
    even = me % 2 == 0

    def flip(a, b):
        out = 0
        bit = 1
        while bit < n_mem:
            out = out + ((a // bit + b // bit) % 2) * bit
            bit *= 2
        return out

    def hop(d, size):
        first = [2, 4, 6, 3, 5, 7, 1]
        second = [4, 2, 7, 5, 3, 6, 1]
        block = d // 8
        r = d % 8
        if r == 0:
            return d
        a = jnp.where(even, first[r - 1], second[r - 1])
        return a + block * 8

    def send(src, dst, send_sem, recv_sem, device):
        copy = pltpu.make_async_remote_copy(
            src_ref=src, dst_ref=dst, send_sem=send_sem, recv_sem=recv_sem,
            device_id=device, device_id_type=MESH,
        )
        copy.start()
        sends.append(copy)

    def arrived(ref, recv_sem):
        pltpu.make_async_remote_copy(
            src_ref=ref, dst_ref=ref, send_sem=kv_send.at[0, 0], recv_sem=recv_sem,
            device_id=((me + 1) % n_mem, z), device_id_type=MESH,
        ).wait_recv()

    def send_kv(kind, source, target):
        for d in range(1, n_mem):
            to = flip(me, hop(d, n_mem))
            send(source.at[:, cols(to % heads)], target.at[src_rows(me)],
                 kv_send.at[kind, d], kv_recv.at[kind, me], (to, z))

    def send_q(s):
        for d in range(1, heads):
            to = flip(j, hop(d, heads))
            send(q_hbm.at[at_rows(turn[s]), cols(to)], q_all.at[j, at_rows(turn[s])],
                 q_send.at[s, d], q_recv.at[s, j], (base + to, z))

    for d in range(1, heads):
        send(p_mine, p_all.at[j], p_send.at[d], p_recv.at[j], (base + (j + d) % heads, z))
    send_kv(0, k_hbm, k_all)
    send_q(0)
    send_kv(1, v_hbm, v_all)
    for s in range(1, min(2, n_head)):
        send_q(s)
    w_copies = []
    for c in range(PIECES):
        span = pl.ds(c * width, width)
        copy = pltpu.make_async_copy(w_hbm.at[:, span], w.at[:, span], w_sem.at[c])
        copy.start()
        w_copies.append(copy)

    def wait_kv(kind, target):
        for d in range(1, n_mem):
            src = (me + n_mem - d) % n_mem
            arrived(target.at[src_rows(src)], kv_recv.at[kind, src])

    scale = math.log2(math.e) / math.sqrt(HD)
    per_tile = HD // rows
    own_backs = []

    def attend(s):
        t = turn[s]
        if s == 0:
            for d in range(1, heads):
                src = (j + heads - d) % heads
                arrived(p_all.at[src], p_recv.at[src])
            locals_[0].wait()
            locals_[1].wait()
            wait_kv(0, k_all)
        for d in range(1, heads):
            src = (j + heads - d) % heads
            arrived(q_all.at[src, at_rows(t)], q_recv.at[s, src])
        lane = lax.broadcasted_iota(jnp.int32, (p_all.shape[1], qdev), 1) // rows
        tiles = []
        for first in range(0, heads, per_tile):
            tile = jnp.zeros((p_all.shape[1], qdev), jnp.int32)
            for k in range(per_tile):
                shift = (k * rows + qdev - t * rows) % qdev
                tile = jnp.where(lane == k, pltpu.roll(p_all[first + k], shift, 1), tile)
            tiles.append(tile)
        probed = jnp.concatenate(tiles, axis=1)
        ids = lax.broadcasted_iota(jnp.int32, (clusters, nq), 0)
        bias = jnp.full((clusters, nq), NEG, jnp.float32)
        for k in range(p_all.shape[1]):
            bias = jnp.where(probed[k : k + 1, :] == ids, 0.0, bias)
        block = q_all[:, at_rows(t), :].reshape(nq, HD)
        scores = lax.dot_general(
            k_all[...], block, (((1,), (1,)), ((), ())), preferred_element_type=jnp.float32
        ) + jnp.dot(onehot[...], bias.astype(jnp.bfloat16), preferred_element_type=jnp.float32)
        peak = jnp.max(scores, axis=0, keepdims=True)
        weights = jnp.exp2((scores - peak) * scale)
        denominator = jnp.sum(weights, axis=0, keepdims=True)
        if s == 0:
            locals_[2].wait()
            wait_kv(1, v_all)
        got = lax.dot_general(
            v_all[...], weights.astype(jnp.bfloat16), (((0,), (0,)), ((), ())),
            preferred_element_type=jnp.float32,
        )
        got = got * (1.0 / denominator)
        o_send[s] = got.T.astype(jnp.bfloat16)
        for d in range(1, heads):
            to = flip(j, hop(d, heads))
            send(o_send.at[s, at_rows(to)], recalled.at[j, at_rows(t)],
                 o_send_sem.at[s, d], o_recv_sem.at[s, j], (base + to, z))
        back = pltpu.make_async_copy(
            o_send.at[s, at_rows(j)], recalled.at[j, at_rows(t)], o_recv_sem.at[s, j])
        back.start()
        own_backs.append(back)
        if s + 2 < n_head:
            send_q(s + 2)

    def project(s):
        t = turn[s]
        own_backs[s].wait()
        for d in range(1, heads):
            src = (j + heads - d) % heads
            arrived(recalled.at[src, at_rows(t)], o_recv_sem.at[s, src])
        if s == 0:
            locals_[3].wait()
        for h in range(heads):
            gate = 1.0 / (1.0 + jnp.exp(-jnp.full((1, HD), gate_ref[h], jnp.float32)))
            mixed = gate * recalled[h, at_rows(t), :].astype(jnp.float32) + (1.0 - gate) * own[
                at_rows(t), h * HD : (h + 1) * HD
            ].astype(jnp.float32)
            blend[:, h * HD : (h + 1) * HD] = mixed.astype(jnp.bfloat16)
        up = t > z
        for c in range(PIECES):
            span = pl.ds(c * width, width)
            if s == 0:
                w_copies[c].wait()
            part[...] = jnp.dot(blend[...], w[:, span], preferred_element_type=jnp.float32)
            if s < n_head - 1:
                has_prev = jnp.where(up, z, n_head - 1 - z) > 0

                @pl.when(has_prev)
                def _():
                    arrived(part_recv.at[t, :, span], r_recv.at[t, c])
                    part[...] += part_recv[t, :, span].astype(jnp.float32)

                part_send[s, :, span] = part[...].astype(jnp.bfloat16)
                to = jnp.where(up, z + 1, z - 1)
                slot = jnp.where(t == z - 1, n_head, t)
                send(part_send.at[s, :, span], part_recv.at[slot, :, span],
                     r_send.at[s, c], r_recv.at[slot, c], (me, to))
            else:

                @pl.when(z > 0)
                def _():
                    arrived(part_recv.at[z, :, span], r_recv.at[z, c])
                    part[...] += part_recv[z, :, span].astype(jnp.float32)

                @pl.when(z < n_head - 1)
                def _():
                    arrived(part_recv.at[n_head, :, span], r_recv.at[n_head, c])
                    part[...] += part_recv[n_head, :, span].astype(jnp.float32)

                out_ref[:, span] = part[...].astype(out_ref.dtype)

    attend(0)
    for s in range(1, n_head):
        attend(s)
        project(s - 1)
    project(n_head - 1)
    for copy in sends:
        copy.wait_send()


def solution(mesh):
    n_mem, n_head = mesh.shape["mem"], mesh.shape["head"]

    def local(queries, mem_keys, mem_values, own_values, gate_bias, w_out, probes, pattern):
        qdev, feats = queries.shape
        kdev = mem_keys.shape[0]
        heads = feats // HD
        width = w_out.shape[1]
        rows = qdev // n_head
        entries = n_mem * kdev
        bf16, f32 = jnp.bfloat16, jnp.float32
        anywhere = pl.BlockSpec(memory_space=pl.ANY)
        smem = pl.BlockSpec(memory_space=pltpu.SMEM)
        vmem = pl.BlockSpec(memory_space=pltpu.VMEM)
        dma = pltpu.SemaphoreType.DMA
        return pl.pallas_call(
            functools.partial(kernel, n_mem, n_head, heads),
            out_shape=jax.ShapeDtypeStruct((rows, width), bf16),
            in_specs=[anywhere, anywhere, anywhere, anywhere, smem, anywhere, vmem, smem],
            out_specs=vmem,
            scratch_shapes=[
                pltpu.VMEM((heads, qdev, HD), bf16),
                pltpu.VMEM((entries, HD), bf16),
                pltpu.VMEM((entries, HD), bf16),
                pltpu.VMEM((heads, probes.shape[1], qdev), jnp.int32),
                pltpu.VMEM((probes.shape[1], qdev), jnp.int32),
                pltpu.VMEM((entries, entries // CSIZE), bf16),
                pltpu.VMEM((n_head, heads * rows, HD), bf16),
                pltpu.VMEM((heads, qdev, HD), bf16),
                pltpu.VMEM((qdev, feats), bf16),
                pltpu.VMEM((feats, width), bf16),
                pltpu.VMEM((rows, feats), bf16),
                pltpu.VMEM((rows, width // PIECES), f32),
                pltpu.VMEM((n_head, rows, width), bf16),
                pltpu.VMEM((n_head + 1, rows, width), bf16),
                dma((2, n_mem)), dma((2, n_mem)),
                dma((n_head, heads)), dma((n_head, heads)),
                dma((n_head, heads)), dma((n_head, heads)),
                dma((heads,)), dma((heads,)),
                dma((n_head, PIECES)), dma((n_head + 1, PIECES)),
                dma((PIECES,)), dma((4,)),
            ],
            compiler_params=pltpu.CompilerParams(
                collective_id=0, has_side_effects=True, vmem_limit_bytes=56 * 2**20
            ),
            cost_estimate=pl.CostEstimate(
                flops=2 * qdev * feats * width, bytes_accessed=2 * feats * width, transcendentals=0
            ),
        )(queries, mem_keys, mem_values, own_values, gate_bias, w_out, probes.T, pattern)

    in_specs = (
        P("mem", "head"),
        P("mem", "head"),
        P("mem", "head"),
        P("mem", "head"),
        P("head"),
        P("head", None),
        P("mem", None),
        P(),
    )
    out_specs = P(("mem", "head"), None)
    return jax.shard_map(local, mesh=mesh, in_specs=in_specs, out_specs=out_specs, check_vma=False)
```
